32 devices in a mesh: groups: 2 (over x), space: 16 (over z, y, core).
Axes of the slice: x: 2, y: 2, z: 4, core: 2. Of those that a mesh axis runs over, the one named last changes fastest.
Arguments:
- grid_latent: bfloat16 [8, 4096, 1024], P(None, ('groups', 'space')), parts along dimension 1, may hold values from -6 to 6
- mesh_latent: bfloat16 [8, 1024, 1024], P(None, ('groups', 'space')), parts along dimension 1, may hold values from -6 to 6
- query_weight: bfloat16 [1024, 1024], replicated, may hold values from -0.1875 to 0.1875
- kv_weight: bfloat16 [1024, 2048], replicated, may hold values from -0.1875 to 0.1875
- field_weight: bfloat16 [100, 1024], replicated, may hold values from -0.1875 to 0.1875
- target: float32 [100, 4096], P(None, ('groups', 'space')), parts along dimension 1, may hold values from -6 to 6
- area_weight: float32 [4096], P(('groups', 'space')), parts along dimension 0, may hold values from 1 to 36
- request: int32 [32, 16, 2], P(('groups', 'space')), parts along dimension 0, may hold values from 0 to 31, as said below
- edge_slot: int32 [3, 4096], P(None, ('groups', 'space')), parts along dimension 1, may hold values from 0 to 31, as said below
Outputs:
- mesh_grad: bfloat16 [8, 1024, 1024], P(None, ('groups', 'space')), parts along dimension 1
- mean_loss: float32 [2], P('groups'), parts along dimension 0
The draws below stay inside these ranges and needn't reach their ends.
There are 2 independent parts, one for each index of `groups`. The reference program is written for one: setup_inputs(seed, part) draws one part's arguments, and reference() takes and returns one part's arrays. A program takes and returns all parts, laid end to end along the dimension named above; an argument that names none is the same for every part. Nothing has to cross between parts.
Inputs may be any that keep to these rules, and one draw needn't show every extreme that they name: request[d, s, 0] and request[d, s, 1] are two different local mesh-node indices of shard s. `edge_slot`: every slot named for shard d = g // 128 indexes that shard's own request row; the 3 slots of one grid point differ; one shard's edges name exactly 16 distinct slots: both slots of 4 source shards, slot 0 of 8 others, none of the rest.
All inputs are finite; a program needn't handle non-finite values.
Results may differ from the reference program's by a relative error of at most 0.0093.
Values may be sent and summed in bfloat16 or wider, within the bound.
A program may use at most 128 MiB of HBM per device.

```python
import math
import jax
import jax.numpy as jnp
from jax import lax

WIDTH = 1024
HEADS = 16
FIELDS = 100
MEMBERS = 8
NEIGH = 3
CAP = 2
GRID_DEV = 128
MESH_DEV = 32
GRID = 2048
MESH = 512
N_SPACE = 16


def plan_edges(key):
    shard_keys = jax.random.split(key, N_SPACE)

    def per_shard(shard_key, shard_index):
        key_order, key_first, key_second, key_points, key_base, key_stride = jax.random.split(shard_key, 6)
        shuffled = jax.random.permutation(key_order, N_SPACE)
        sources = (shard_index + N_SPACE // 2 + (shuffled - shuffled[0]) % N_SPACE) % N_SPACE
        quarter_count = N_SPACE // 4
        doubled = sources[:quarter_count] * CAP
        used_slots = jnp.concatenate([doubled, doubled + 1, sources[quarter_count:3 * quarter_count] * CAP])
        first_node = jax.random.randint(key_first, (N_SPACE,), 0, MESH_DEV)
        second_node = (first_node + 1 + jax.random.randint(key_second, (N_SPACE,), 0, MESH_DEV - 1)) % MESH_DEV
        requested = jnp.stack([first_node, second_node], axis=1)
        ordering = jax.random.permutation(key_points, GRID_DEV)
        base_slot = jnp.where(ordering < N_SPACE, ordering, jax.random.randint(key_base, (GRID_DEV,), 0, N_SPACE))
        stride_step = jax.random.randint(key_stride, (GRID_DEV,), 1, (N_SPACE - 1) // 2 + 1)
        picked = (base_slot[None, :] + jnp.arange(NEIGH)[:, None] * stride_step[None, :]) % N_SPACE
        return (requested, used_slots[picked])
    requested, edge_table = jax.vmap(per_shard)(shard_keys, jnp.arange(N_SPACE))
    requested = requested.at[0, 0, 0].set(MESH_DEV - 1).at[0, 0, 1].set(0)
    edge_table = edge_table.transpose(1, 0, 2).reshape(NEIGH, N_SPACE * GRID_DEV)
    return (requested.astype(jnp.int32), edge_table.astype(jnp.int32))


def draw_request(key, part):
    requested, edge_table = plan_edges(key)
    return requested


def draw_edge_slot(key, part):
    requested, edge_table = plan_edges(key)
    return edge_table


def draw_area_weight(key, part):
    key = jax.random.fold_in(key, 11)
    position = jnp.arange(GRID, dtype=jnp.float32) / GRID
    return (1.0 + 2.0 * position) * jnp.exp(jax.random.uniform(key, (GRID,), jnp.float32, 0.0, math.log(4.0)))


def levels(rng, extent, cuts, least, top_value):
    def one(dim, shards_of):
        heights = jax.random.uniform(jax.random.fold_in(jax.random.fold_in(rng, 6), dim), (shards_of,), jnp.float32, least / len(cuts), top_value / len(cuts))
        return jnp.repeat(jnp.exp(heights), extent[dim] // shards_of).reshape((-1,) + (1,) * (len(extent) - dim - 1))

    factor_of = one(*cuts[0])
    for cut in cuts[1:]:
        factor_of = factor_of * one(*cut)
    return factor_of


def bell_draw(stream_key, dims, deviation, reach, cuts=(), kind=jnp.bfloat16):
    drawn = deviation * jax.random.normal(stream_key, dims, jnp.float32)
    if cuts:
        drawn = drawn * levels(stream_key, dims, cuts, -0.22, 0.18)
    return jnp.clip(drawn, -reach, reach).astype(kind)


def setup_inputs(seed: int = 0, part: int = 0) -> dict:
    key_list = jax.random.split(jax.random.key(seed), 10)
    part_keys = jax.random.split(jax.random.fold_in(key_list[9], part), 10)
    grid_latent = bell_draw(part_keys[0], (MEMBERS, GRID, WIDTH), 1.0, 6.0, ((1, 16),))
    mesh_latent = bell_draw(part_keys[1], (MEMBERS, MESH, WIDTH), 1.0, 6.0, ((1, 16),))
    query_weight = bell_draw(key_list[2], (WIDTH, WIDTH), WIDTH ** -0.5, 0.1875)
    kv_weight = bell_draw(key_list[3], (WIDTH, 2 * WIDTH), WIDTH ** -0.5, 0.1875)
    field_weight = bell_draw(key_list[4], (FIELDS, WIDTH), WIDTH ** -0.5, 0.1875)
    target = bell_draw(part_keys[5], (FIELDS, GRID), 1.0, 6.0, ((1, 16),), jnp.float32)
    area_weight = draw_area_weight(jax.random.fold_in(jax.random.fold_in(key_list[9], part), 71), part)
    request = draw_request(jax.random.fold_in(jax.random.fold_in(key_list[9], part), 71), part)
    edge_slot = draw_edge_slot(jax.random.fold_in(jax.random.fold_in(key_list[9], part), 71), part)
    return dict(grid_latent=grid_latent, mesh_latent=mesh_latent, query_weight=query_weight, kv_weight=kv_weight, field_weight=field_weight, target=target, area_weight=area_weight, request=request, edge_slot=edge_slot)


SMOOTHING = 0.04
FAIRNESS = 0.95

def rounded(values):
    narrow = lax.optimization_barrier(values.astype(jnp.bfloat16)).astype(jnp.float32)
    return values + lax.stop_gradient(narrow - values)

def member_attention(queries, slot_kv, edge_slot):
    model_width = queries.shape[1]
    head_dim = model_width // HEADS
    point_count = edge_slot.shape[1]
    kv_table = slot_kv.astype(jnp.float32)
    edge_rows = jnp.take(kv_table, edge_slot, axis=0)
    key_heads = edge_rows[:, :, :model_width].reshape(NEIGH, point_count, HEADS, head_dim)
    value_heads = edge_rows[:, :, model_width:].reshape(NEIGH, point_count, HEADS, head_dim)
    query_heads = queries.astype(jnp.float32).reshape(1, point_count, HEADS, head_dim)
    scores = lax.optimization_barrier(jnp.sum(key_heads * query_heads, axis=3)) / math.sqrt(head_dim)
    exponent = jnp.exp(scores)
    weights = rounded(exponent / lax.optimization_barrier(jnp.sum(exponent, axis=0, keepdims=True)))
    attended = lax.optimization_barrier(jnp.sum(weights[..., None] * value_heads, axis=0)).reshape(point_count, model_width)
    return rounded(attended)

def smooth(difference):
    return jnp.sqrt(difference * difference + SMOOTHING)

def grid_total(queries, slot_kv, edge_slot, field_weight, target, area_weight):
    attended = lax.map(lambda member_pair: member_attention(member_pair[0], member_pair[1], edge_slot), (queries, slot_kv))
    predict = jnp.einsum('egd,fd->efg', attended, field_weight.astype(jnp.float32), precision=lax.Precision.HIGHEST)
    members = predict.shape[0]
    skill_term = lax.optimization_barrier(jnp.mean(smooth(predict - target[None]), axis=0))
    spread = lax.optimization_barrier(jnp.sum(smooth(predict[:, None] - predict[None, :]), axis=(0, 1))) - members * math.sqrt(SMOOTHING)
    almost_fair = 1.0 - (1.0 - FAIRNESS) / members
    pointwise = skill_term - almost_fair * spread / (2.0 * members * (members - 1))
    return jnp.sum(pointwise * area_weight[None, :])

def reference(grid_latent, mesh_latent, query_weight, kv_weight, field_weight, target, area_weight, request, edge_slot):
    member_count, grid_count, model_width = grid_latent.shape
    mesh_count = mesh_latent.shape[1]
    queries = jnp.dot(grid_latent.reshape(member_count * grid_count, model_width), query_weight, preferred_element_type=jnp.float32)
    queries = queries.astype(jnp.bfloat16).reshape(member_count, grid_count, model_width)
    node_kv = jnp.dot(mesh_latent.reshape(member_count * mesh_count, model_width), kv_weight, preferred_element_type=jnp.float32)
    node_kv = node_kv.astype(jnp.bfloat16).reshape(member_count, mesh_count, 2 * model_width)
    shard_base = jnp.arange(N_SPACE, dtype=jnp.int32)[:, None] * MESH_DEV
    slot_total = N_SPACE * CAP

    def shard_step(gradient_sum, shard_index):
        first_row = (shard_index * GRID_DEV).astype(jnp.int32)
        own_queries = lax.dynamic_slice_in_dim(queries, first_row, GRID_DEV, 1)
        own_target = lax.dynamic_slice_in_dim(target, first_row, GRID_DEV, 1)
        own_weight = lax.dynamic_slice_in_dim(area_weight, first_row, GRID_DEV, 0)
        own_edges = lax.dynamic_slice_in_dim(edge_slot, first_row, GRID_DEV, 1)
        wanted = (shard_base + request[shard_index]).reshape(-1).astype(jnp.int32)
        slot_kv = jnp.take(node_kv, wanted, axis=1)
        shard_total, pullback = jax.vjp(lambda slot_rows: grid_total(own_queries, slot_rows, own_edges, field_weight, own_target, own_weight), slot_kv)
        slot_grad, = pullback(jnp.ones((), shard_total.dtype))
        slot_grad = slot_grad.astype(jnp.bfloat16).reshape(member_count * slot_total, 2 * model_width)
        slot_latent = jnp.dot(slot_grad, kv_weight.T, preferred_element_type=jnp.float32).astype(jnp.bfloat16)
        slot_latent = slot_latent.reshape(member_count, slot_total, model_width)
        gradient_sum = gradient_sum.at[:, wanted].add(slot_latent.astype(jnp.float32))
        return (gradient_sum, shard_total)
    start_grad = jnp.zeros((member_count, mesh_count, model_width), jnp.float32)
    node_grad, totals = lax.scan(shard_step, start_grad, jnp.arange(N_SPACE, dtype=jnp.int32))
    mesh_grad = node_grad.astype(jnp.bfloat16)
    mean_loss = (jnp.sum(totals) / (FIELDS * grid_count)).reshape(1)
    return (mesh_grad, mean_loss)
```

```python
import functools
import math

import jax
import jax.numpy as jnp
from jax import lax
from jax.experimental import pallas as pl
from jax.experimental.pallas import tpu as pltpu
from jax.sharding import PartitionSpec as P

HEADS = 16
SMOOTHING = 0.04
FAIRNESS = 0.95
BF = jnp.bfloat16
F32 = jnp.float32


def dot(a, b, dims):
    return lax.dot_general(a, b, ((dims[:1], dims[1:]), ((), ())), preferred_element_type=F32)


def iota(shape, dim):
    return lax.broadcasted_iota(jnp.int32, shape, dim)


def order_matrix(rows, members, slots, cap):
    r, c = iota((rows, rows), 0), iota((rows, rows), 1)
    member, slot = r // slots, r % slots
    return (c == slot * members + member).astype(F32).astype(BF)


def decoder_kernel(
    members, fields, slots, cap,
    x_ref, lat_ref, qw_ref, kvw_ref, fw_ref, target_ref, area_ref, edge_ref,
    out_ref, total_ref,
    q_s, kv_s, p_s, att_s, pred_s, dp_s, da_s, sg_s,
):
    points = target_ref.shape[1]
    width = qw_ref.shape[0]
    rows = members * slots
    head_dim = width // HEADS
    group_heads = 256 // head_dim
    groups = HEADS // group_heads
    order = order_matrix(rows, members, slots, cap)
    latent = dot(order, lat_ref[...], (1, 0)).astype(BF)
    for c in range(0, 2 * width, 512):
        kv_s[:, c:c + 512] = dot(latent, kvw_ref[:, c:c + 512], (1, 0)).astype(BF)
    for c in range(0, width, 256):
        q_s[:, c:c + 256] = dot(x_ref[...], qw_ref[:, c:c + 256], (1, 0)).astype(BF)

    hs = group_heads * slots
    head_mask = (iota((hs, 256), 0) // slots == iota((hs, 256), 1) // head_dim).astype(F32)
    head_mask16 = head_mask.astype(BF)
    slot_ids = iota((slots, points), 0)
    named = (slot_ids == edge_ref[0:1, :]) | (slot_ids == edge_ref[1:2, :]) | (slot_ids == edge_ref[2:3, :])
    named = named.astype(F32)
    named = jnp.concatenate([named] * group_heads, axis=0) > 0.5

    def blocks(values):
        return jnp.concatenate([values] * group_heads, axis=0) * head_mask16

    scale = 1.0 / math.sqrt(head_dim)
    for e in range(members):
        rs = slice(e * slots, (e + 1) * slots)
        gs = slice(e * points, (e + 1) * points)
        for k in range(groups):
            cs = slice(k * 256, (k + 1) * 256)
            keys = blocks(kv_s[rs, cs])
            values = blocks(kv_s[rs, width + k * 256:width + (k + 1) * 256])
            score = dot(keys, q_s[gs, cs], (1, 1)) * scale
            exponent = jnp.where(named, jnp.exp(score), 0.0)
            by_head = exponent.reshape(group_heads, slots, points)
            total = jnp.sum(by_head, axis=1, keepdims=True)
            weight = (by_head / total).reshape(hs, points)
            p_s[e, k] = weight
            att_s[cs, gs] = dot(values, weight.astype(BF), (0, 0)).astype(BF)

    pred_s[...] = dot(fw_ref[...], att_s[...], (1, 0))

    area = area_ref[...]
    almost_fair = 1.0 - (1.0 - FAIRNESS) / members
    spread_factor = almost_fair / (members * (members - 1))
    total = jnp.zeros((8, points), F32)
    padded = fw_ref.shape[0]
    for f in range(0, padded, 8):
        fs = slice(f, f + 8)
        if f >= fields:
            dp_s[fs, :] = jnp.zeros((8, members * points), F32)
            continue
        goal = target_ref[fs, :]
        preds = [pred_s[fs, e * points:(e + 1) * points] for e in range(members)]
        slopes = []
        skill = jnp.zeros((8, points), F32)
        for e in range(members):
            u = preds[e] - goal
            v = u * u + SMOOTHING
            r = lax.rsqrt(v)
            skill += v * r
            slopes.append(u * r * (1.0 / members))
        spread = jnp.zeros((8, points), F32)
        pulls = [jnp.zeros((8, points), F32) for _ in range(members)]
        for a in range(members):
            for b in range(a + 1, members):
                u = preds[a] - preds[b]
                v = u * u + SMOOTHING
                r = lax.rsqrt(v)
                spread += v * r
                w = u * r
                pulls[a] = pulls[a] + w
                pulls[b] = pulls[b] - w
        pointwise = skill * (1.0 / members) - spread_factor * spread
        valid = iota((8, points), 0) + f < fields
        total += jnp.where(valid, pointwise * area, 0.0)
        for e in range(members):
            slope = (slopes[e] - spread_factor * pulls[e]) * area
            dp_s[fs, e * points:(e + 1) * points] = jnp.where(valid, slope, 0.0)
    total_ref[...] = total

    dp = dp_s[...].astype(BF)
    for k in range(groups):
        cs = slice(k * 256, (k + 1) * 256)
        da_s[cs, :] = dot(fw_ref[:, cs], dp, (0, 0)).astype(BF)

    def fold(product):
        kept = (product * head_mask).reshape(group_heads, slots, 256)
        return jnp.sum(kept, axis=0).astype(BF)

    for e in range(members):
        rs = slice(e * slots, (e + 1) * slots)
        gs = slice(e * points, (e + 1) * points)
        for k in range(groups):
            cs = slice(k * 256, (k + 1) * 256)
            vs = slice(width + k * 256, width + (k + 1) * 256)
            values = blocks(kv_s[rs, vs])
            weight = p_s[e, k]
            da = da_s[cs, gs]
            dw = dot(values, da, (1, 0))
            pull = (weight * dw).reshape(group_heads, slots, points)
            mean = jnp.sum(pull, axis=1, keepdims=True)
            ds = pull - weight.reshape(group_heads, slots, points) * mean
            ds = (ds.reshape(hs, points) * scale).astype(BF)
            sg_s[rs, cs] = fold(dot(ds, q_s[gs, cs], (1, 0)))
            sg_s[rs, vs] = fold(dot(weight.astype(BF), da, (1, 1)))

    latent_grad = dot(sg_s[...], kvw_ref[...], (1, 1)).astype(BF)
    out_ref[...] = dot(order, latent_grad, (0, 0)).astype(BF)


def decode(grid_latent, latent, query_weight, kv_weight, field_weight, target, area, edge_slot, members, slots, cap, fields):
    points, width = target.shape[1], query_weight.shape[0]
    padded = field_weight.shape[0]
    rows = members * slots
    group_heads = 256 * HEADS // width
    vmem = pl.BlockSpec(memory_space=pltpu.VMEM)
    return pl.pallas_call(
        functools.partial(decoder_kernel, members, fields, slots, cap),
        out_shape=(
            jax.ShapeDtypeStruct((rows, width), BF),
            jax.ShapeDtypeStruct((8, points), F32),
        ),
        in_specs=[vmem] * 8,
        out_specs=(vmem, vmem),
        scratch_shapes=[
            pltpu.VMEM((members * points, width), BF),
            pltpu.VMEM((rows, 2 * width), BF),
            pltpu.VMEM((members, HEADS // group_heads, group_heads * slots, points), F32),
            pltpu.VMEM((width, members * points), BF),
            pltpu.VMEM((padded, members * points), F32),
            pltpu.VMEM((padded, members * points), F32),
            pltpu.VMEM((width, members * points), BF),
            pltpu.VMEM((rows, 2 * width), BF),
        ],
        compiler_params=pltpu.CompilerParams(vmem_limit_bytes=56 * 1024 * 1024),
    )(grid_latent, latent, query_weight, kv_weight, field_weight, target, area, edge_slot)


def local(
    grid_latent, mesh_latent, query_weight, kv_weight, field_weight, target, area_weight, request, edge_slot,
):
    members, points, width = grid_latent.shape
    nodes = mesh_latent.shape[1]
    shards = lax.axis_size("space")
    cap = request.shape[2]
    slots = shards * cap
    per = cap * members
    fields = target.shape[0]
    incoming = lax.all_to_all(request.reshape(shards, cap), "space", split_axis=0, concat_axis=0, tiled=True)
    wanted = jnp.broadcast_to(incoming[:, :, None], (shards, cap, members)).reshape(shards * per, 1)
    member_of = iota((shards * per, members * nodes), 0) % members
    column = iota((shards * per, members * nodes), 1)
    select = (column == member_of * nodes + wanted).astype(BF)
    rows = mesh_latent.reshape(members * nodes, width)
    picked = jnp.dot(select, rows, preferred_element_type=F32).astype(BF)
    arrived = lax.all_to_all(
        picked.reshape(shards, per, width), "space", split_axis=0, concat_axis=0, tiled=True
    ).reshape(shards * per, width)
    field_pad = jnp.pad(field_weight, ((0, 128 - fields), (0, 0)))
    target_pad = jnp.pad(target, ((0, -fields % 8), (0, 0)))
    grads, total = decode(
        grid_latent.reshape(members * points, width), arrived, query_weight, kv_weight, field_pad,
        target_pad, area_weight.reshape(1, points), edge_slot, members, slots, cap, fields,
    )
    returned = lax.all_to_all(
        grads.reshape(shards, per, width), "space", split_axis=0, concat_axis=0, tiled=True
    ).reshape(shards * per, width)
    mesh_grad = lax.dot_general(
        select, returned, (((0,), (0,)), ((), ())), preferred_element_type=F32
    ).astype(BF).reshape(members, nodes, width)
    totals = lax.all_to_all(
        jnp.broadcast_to(jnp.sum(total), (shards, 128)), "space", split_axis=0, concat_axis=0, tiled=True
    )
    mean_loss = (jnp.sum(totals[:, 0]) / (fields * points * shards)).reshape(1)
    return (mesh_grad, mean_loss)


def solution(mesh):
    placed = (
        P(None, ("groups", "space"), None),
        P(None, ("groups", "space"), None),
        P(),
        P(),
        P(),
        P(None, ("groups", "space")),
        P(("groups", "space")),
        P(("groups", "space"), None, None),
        P(None, ("groups", "space")),
    )
    return jax.shard_map(
        local,
        mesh=mesh,
        in_specs=placed,
        out_specs=(P(None, ("groups", "space"), None), P("groups")),
        check_vma=False,
    )
```

```python
import functools
import math

import jax
import jax.numpy as jnp
from jax import lax
from jax.experimental import pallas as pl
from jax.experimental.pallas import tpu as pltpu
from jax.sharding import PartitionSpec as P

HEADS = 16
SMOOTHING = 0.04
FAIRNESS = 0.95
BF = jnp.bfloat16
F32 = jnp.float32


def dot(a, b, dims):
    return lax.dot_general(a, b, ((dims[:1], dims[1:]), ((), ())), preferred_element_type=F32)


def iota(shape, dim):
    return lax.broadcasted_iota(jnp.int32, shape, dim)


def order_matrix(rows, members, slots, cap):
    r, c = iota((rows, rows), 0), iota((rows, rows), 1)
    member, slot = r // slots, r % slots
    return (c == slot * members + member).astype(F32).astype(BF)


def decoder_kernel(
    members, fields, slots, cap,
    q_s, lat_ref, kvw_ref, fw_ref, target_ref, area_ref, edge_ref,
    out_ref, total_ref,
    kv_s, p_s, att_s, pred_s, dp_s, da_s, sg_s,
):
    points = target_ref.shape[1]
    width = kvw_ref.shape[0]
    rows = members * slots
    head_dim = width // HEADS
    group_heads = 256 // head_dim
    groups = HEADS // group_heads
    order = order_matrix(rows, members, slots, cap)
    latent = dot(order, lat_ref[...], (1, 0)).astype(BF)
    for c in range(0, 2 * width, 512):
        kv_s[:, c:c + 512] = dot(latent, kvw_ref[:, c:c + 512], (1, 0)).astype(BF)

    hs = group_heads * slots
    head_mask = (iota((hs, 256), 0) // slots == iota((hs, 256), 1) // head_dim).astype(F32)
    head_mask16 = head_mask.astype(BF)
    slot_ids = iota((slots, points), 0)
    named = (slot_ids == edge_ref[0:1, :]) | (slot_ids == edge_ref[1:2, :]) | (slot_ids == edge_ref[2:3, :])
    named = named.astype(F32)
    named = jnp.concatenate([named] * group_heads, axis=0) > 0.5

    def blocks(values):
        return jnp.concatenate([values] * group_heads, axis=0) * head_mask16

    scale = 1.0 / math.sqrt(head_dim)
    for e in range(members):
        rs = slice(e * slots, (e + 1) * slots)
        gs = slice(e * points, (e + 1) * points)
        for k in range(groups):
            cs = slice(k * 256, (k + 1) * 256)
            keys = blocks(kv_s[rs, cs])
            values = blocks(kv_s[rs, width + k * 256:width + (k + 1) * 256])
            score = dot(keys, q_s[gs, cs], (1, 1)) * scale
            exponent = jnp.where(named, jnp.exp(score), 0.0)
            by_head = exponent.reshape(group_heads, slots, points)
            total = jnp.sum(by_head, axis=1, keepdims=True)
            weight = (by_head / total).reshape(hs, points)
            p_s[e, k] = weight
            att_s[cs, gs] = dot(values, weight.astype(BF), (0, 0)).astype(BF)

    pred_s[...] = dot(fw_ref[...], att_s[...], (1, 0))

    area = area_ref[...]
    almost_fair = 1.0 - (1.0 - FAIRNESS) / members
    spread_factor = almost_fair / (members * (members - 1))
    total = jnp.zeros((8, points), F32)
    padded = fw_ref.shape[0]
    for f in range(0, padded, 8):
        fs = slice(f, f + 8)
        if f >= fields:
            dp_s[fs, :] = jnp.zeros((8, members * points), F32)
            continue
        goal = target_ref[fs, :]
        preds = [pred_s[fs, e * points:(e + 1) * points] for e in range(members)]
        slopes = []
        skill = jnp.zeros((8, points), F32)
        for e in range(members):
            u = preds[e] - goal
            v = u * u + SMOOTHING
            r = lax.rsqrt(v)
            skill += v * r
            slopes.append(u * r * (1.0 / members))
        spread = jnp.zeros((8, points), F32)
        pulls = [jnp.zeros((8, points), F32) for _ in range(members)]
        for a in range(members):
            for b in range(a + 1, members):
                u = preds[a] - preds[b]
                v = u * u + SMOOTHING
                r = lax.rsqrt(v)
                spread += v * r
                w = u * r
                pulls[a] = pulls[a] + w
                pulls[b] = pulls[b] - w
        pointwise = skill * (1.0 / members) - spread_factor * spread
        valid = iota((8, points), 0) + f < fields
        total += jnp.where(valid, pointwise * area, 0.0)
        for e in range(members):
            slope = (slopes[e] - spread_factor * pulls[e]) * area
            dp_s[fs, e * points:(e + 1) * points] = jnp.where(valid, slope, 0.0)
    total_ref[...] = total

    dp = dp_s[...].astype(BF)
    for k in range(groups):
        cs = slice(k * 256, (k + 1) * 256)
        da_s[cs, :] = dot(fw_ref[:, cs], dp, (0, 0)).astype(BF)

    def fold(product):
        kept = (product * head_mask).reshape(group_heads, slots, 256)
        return jnp.sum(kept, axis=0).astype(BF)

    for e in range(members):
        rs = slice(e * slots, (e + 1) * slots)
        gs = slice(e * points, (e + 1) * points)
        for k in range(groups):
            cs = slice(k * 256, (k + 1) * 256)
            vs = slice(width + k * 256, width + (k + 1) * 256)
            values = blocks(kv_s[rs, vs])
            weight = p_s[e, k]
            da = da_s[cs, gs]
            dw = dot(values, da, (1, 0))
            pull = (weight * dw).reshape(group_heads, slots, points)
            mean = jnp.sum(pull, axis=1, keepdims=True)
            ds = pull - weight.reshape(group_heads, slots, points) * mean
            ds = (ds.reshape(hs, points) * scale).astype(BF)
            sg_s[rs, cs] = fold(dot(ds, q_s[gs, cs], (1, 0)))
            sg_s[rs, vs] = fold(dot(weight.astype(BF), da, (1, 1)))

    latent_grad = dot(sg_s[...], kvw_ref[...], (1, 1)).astype(BF)
    out_ref[...] = dot(order, latent_grad, (0, 0)).astype(BF)


def decode(queries, latent, kv_weight, field_weight, target, area, edge_slot, members, slots, cap, fields):
    points, width = target.shape[1], kv_weight.shape[0]
    padded = field_weight.shape[0]
    rows = members * slots
    group_heads = 256 * HEADS // width
    vmem = pl.BlockSpec(memory_space=pltpu.VMEM)
    return pl.pallas_call(
        functools.partial(decoder_kernel, members, fields, slots, cap),
        out_shape=(
            jax.ShapeDtypeStruct((rows, width), BF),
            jax.ShapeDtypeStruct((8, points), F32),
        ),
        in_specs=[vmem] * 7,
        out_specs=(vmem, vmem),
        scratch_shapes=[
            pltpu.VMEM((rows, 2 * width), BF),
            pltpu.VMEM((members, HEADS // group_heads, group_heads * slots, points), F32),
            pltpu.VMEM((width, members * points), BF),
            pltpu.VMEM((padded, members * points), F32),
            pltpu.VMEM((padded, members * points), F32),
            pltpu.VMEM((width, members * points), BF),
            pltpu.VMEM((rows, 2 * width), BF),
        ],
        compiler_params=pltpu.CompilerParams(vmem_limit_bytes=56 * 1024 * 1024),
    )(queries, latent, kv_weight, field_weight, target, area, edge_slot)


def greet(shards, me):
    barrier = pltpu.get_barrier_semaphore()

    def tell(step, carry):
        partner = lax.rem(me + step, shards)
        pl.semaphore_signal(barrier, inc=1, device_id={"space": partner}, device_id_type=pl.DeviceIdType.MESH)
        return carry

    lax.fori_loop(1, shards, tell, 0)
    pl.semaphore_wait(barrier, shards - 1)


def part(index, size):
    return pl.ds(pl.multiple_of(index * size, size), size)


def exchange(shards, me, size, src, dst, send_sem, recv_sem, whole=False):
    def copy(partner, landing):
        return pltpu.make_async_remote_copy(
            src_ref=src if whole else src.at[part(partner, size)],
            dst_ref=dst.at[part(landing, size)],
            send_sem=send_sem.at[partner],
            recv_sem=recv_sem.at[landing],
            device_id={"space": partner},
            device_id_type=pl.DeviceIdType.MESH,
        )

    def start(step, carry):
        copy(lax.rem(me + step, shards), me).start()
        return carry

    def finish(step, carry):
        copy(lax.rem(me + step, shards), me).wait_send()
        sender = lax.rem(me + shards - step, shards)
        copy(sender, sender).wait_recv()
        return carry

    lax.fori_loop(1, shards, start, 0)
    return lambda: lax.fori_loop(1, shards, finish, 0)


def selection(got, members, nodes):
    member = iota(got.shape, 0) % members
    lane = iota(got.shape, 1)
    parts = [
        (lane + c == member * nodes + got).astype(F32).astype(BF)
        for c in range(0, members * nodes, 128)
    ]
    return jnp.concatenate(parts, axis=1)


def gather_kernel(
    shards, members, nodes,
    ask_ref, mesh_ref, x_ref, qw_ref, got_ref, q_ref, arrived_ref,
    got_s, picked_s, arrived_s, ask_send, ask_recv, row_send, row_recv,
):
    me = lax.axis_index("space")
    per = ask_ref.shape[0] // shards
    width = mesh_ref.shape[1]

    def project(first, last):
        for c in range(first, last, 256):
            q_ref[:, c:c + 256] = dot(x_ref[...], qw_ref[:, c:c + 256], (1, 0)).astype(BF)

    greet(shards, me)
    finish = exchange(shards, me, per, ask_ref, got_s, ask_send, ask_recv)
    got_s[part(me, per), :] = ask_ref[part(me, per), :]
    project(0, width // 2)
    finish()
    got = got_s[...]
    got_ref[...] = got
    picked_s[...] = dot(selection(got, members, nodes), mesh_ref[...], (1, 0)).astype(BF)
    finish = exchange(shards, me, per, picked_s, arrived_s, row_send, row_recv)
    arrived_s[part(me, per), :] = picked_s[part(me, per), :]
    project(width // 2, width)
    finish()
    arrived_ref[...] = arrived_s[...]


def gather_rows(ask, mesh_rows, x, query_weight, shards, members, nodes):
    rows, width = ask.shape[0], mesh_rows.shape[1]
    vmem = pl.BlockSpec(memory_space=pltpu.VMEM)
    sems = pltpu.SemaphoreType.DMA((shards,))
    return pl.pallas_call(
        functools.partial(gather_kernel, shards, members, nodes),
        out_shape=(
            jax.ShapeDtypeStruct(ask.shape, jnp.int32),
            jax.ShapeDtypeStruct(x.shape, BF),
            jax.ShapeDtypeStruct((rows, width), BF),
        ),
        in_specs=[vmem] * 4,
        out_specs=(vmem, vmem, vmem),
        scratch_shapes=[
            pltpu.VMEM(ask.shape, jnp.int32),
            pltpu.VMEM((rows, width), BF),
            pltpu.VMEM((rows, width), BF),
            sems, sems, sems, sems,
        ],
        compiler_params=pltpu.CompilerParams(
            collective_id=0, has_side_effects=True, vmem_limit_bytes=40 * 1024 * 1024
        ),
    )(ask, mesh_rows, x, query_weight)


def return_kernel(
    shards, members, nodes, count,
    got_ref, grads_ref, total_ref, out_ref, loss_ref,
    back_s, totals_s, row_send, row_recv, total_send, total_recv,
):
    me = lax.axis_index("space")
    per = grads_ref.shape[0] // shards
    greet(shards, me)
    finish = exchange(shards, me, per, grads_ref, back_s, row_send, row_recv)
    finish_total = exchange(shards, me, 8, total_ref, totals_s, total_send, total_recv, whole=True)
    back_s[part(me, per), :] = grads_ref[part(me, per), :]
    totals_s[part(me, 8), :] = total_ref[...]
    select = selection(got_ref[...], members, nodes)
    finish()
    finish_total()
    out_ref[...] = dot(select, back_s[...], (0, 0)).astype(BF)
    loss_ref[...] = jnp.full(loss_ref.shape, 1.0, F32) * (jnp.sum(totals_s[...]) / count)


def return_rows(got, grads, total, shards, members, nodes, count):
    rows, width = grads.shape
    vmem = pl.BlockSpec(memory_space=pltpu.VMEM)
    sems = pltpu.SemaphoreType.DMA((shards,))
    return pl.pallas_call(
        functools.partial(return_kernel, shards, members, nodes, count),
        out_shape=(
            jax.ShapeDtypeStruct((members * nodes, width), BF),
            jax.ShapeDtypeStruct((8, 128), F32),
        ),
        in_specs=[vmem] * 3,
        out_specs=(vmem, vmem),
        scratch_shapes=[
            pltpu.VMEM((rows, width), BF),
            pltpu.VMEM((shards * 8, total.shape[1]), F32),
            sems, sems, sems, sems,
        ],
        compiler_params=pltpu.CompilerParams(
            collective_id=1, has_side_effects=True, vmem_limit_bytes=40 * 1024 * 1024
        ),
    )(got, grads, total)


def local(
    grid_latent, mesh_latent, query_weight, kv_weight, field_weight, target, area_weight, request, edge_slot,
):
    members, points, width = grid_latent.shape
    nodes = mesh_latent.shape[1]
    shards = lax.axis_size("space")
    cap = request.shape[2]
    slots = shards * cap
    per = cap * members
    fields = target.shape[0]
    ask = jnp.broadcast_to(
        request.reshape(slots, 1, 1), (slots, members, 128)
    ).reshape(shards * per, 128)
    got, queries, arrived = gather_rows(
        ask, mesh_latent.reshape(members * nodes, width), grid_latent.reshape(members * points, width),
        query_weight, shards, members, nodes,
    )
    field_pad = jnp.pad(field_weight, ((0, 128 - fields), (0, 0)))
    target_pad = jnp.pad(target, ((0, -fields % 8), (0, 0)))
    grads, total = decode(
        queries, arrived, kv_weight, field_pad, target_pad, area_weight.reshape(1, points), edge_slot,
        members, slots, cap, fields,
    )
    mesh_grad, loss = return_rows(
        got, grads, total, shards, members, nodes, float(fields * points * shards)
    )
    mesh_grad = mesh_grad.reshape(members, nodes, width)
    mean_loss = loss[0, 0:1]
    return (mesh_grad, mean_loss)


def solution(mesh):
    placed = (
        P(None, ("groups", "space"), None),
        P(None, ("groups", "space"), None),
        P(),
        P(),
        P(),
        P(None, ("groups", "space")),
        P(("groups", "space")),
        P(("groups", "space"), None, None),
        P(None, ("groups", "space")),
    )
    return jax.shard_map(
        local,
        mesh=mesh,
        in_specs=placed,
        out_specs=(P(None, ("groups", "space"), None), P("groups")),
        check_vma=False,
    )
```

```python
import functools
import math

import jax
import jax.numpy as jnp
from jax import lax
from jax.experimental import pallas as pl
from jax.experimental.pallas import tpu as pltpu
from jax.sharding import PartitionSpec as P

HEADS = 16
SMOOTHING = 0.04
FAIRNESS = 0.95
BF = jnp.bfloat16
F32 = jnp.float32


def dot(a, b, dims):
    return lax.dot_general(a, b, ((dims[:1], dims[1:]), ((), ())), preferred_element_type=F32)


def iota(shape, dim):
    return lax.broadcasted_iota(jnp.int32, shape, dim)


def order_matrix(rows, members, slots, cap):
    r, c = iota((rows, rows), 0), iota((rows, rows), 1)
    member, slot = r // slots, r % slots
    return (c == slot * members + member).astype(F32).astype(BF)


def greet(shards, me):
    barrier = pltpu.get_barrier_semaphore()

    def tell(step, carry):
        partner = lax.rem(me + step, shards)
        pl.semaphore_signal(barrier, inc=1, device_id={"space": partner}, device_id_type=pl.DeviceIdType.MESH)
        return carry

    lax.fori_loop(1, shards, tell, 0)
    pl.semaphore_wait(barrier, shards - 1)


def part(index, size):
    return pl.ds(pl.multiple_of(index * size, size), size)


def exchange(shards, me, size, src, dst, send_sem, recv_sem, whole=False):
    def copy(partner, landing):
        return pltpu.make_async_remote_copy(
            src_ref=src if whole else src.at[part(partner, size)],
            dst_ref=dst.at[part(landing, size)],
            send_sem=send_sem.at[partner],
            recv_sem=recv_sem.at[landing],
            device_id={"space": partner},
            device_id_type=pl.DeviceIdType.MESH,
        )

    def start(step, carry):
        copy(lax.rem(me + step, shards), me).start()
        return carry

    def finish(step, carry):
        copy(lax.rem(me + step, shards), me).wait_send()
        sender = lax.rem(me + shards - step, shards)
        copy(sender, sender).wait_recv()
        return carry

    lax.fori_loop(1, shards, start, 0)
    return lambda: lax.fori_loop(1, shards, finish, 0)


def selection(got, members, nodes):
    member = iota(got.shape, 0) % members
    lane = iota(got.shape, 1)
    parts = [
        (lane + c == member * nodes + got).astype(F32).astype(BF)
        for c in range(0, members * nodes, 128)
    ]
    return jnp.concatenate(parts, axis=1)


def decoder_kernel(
    shards, members, fields, slots, cap, nodes, count,
    ask_ref, mesh_ref, fw_ref, target_ref, area_ref, edge_ref, x_hbm, qw_hbm, kvw_hbm,
    out_ref, loss_ref,
    x_s, qw_s, kvw_s, got_s, picked_s, arrived_s, grads_s, back_s, total_s, totals_s,
    q_s, kv_s, p_s, att_s, target_s, pred_s, dp_s, da_s, sg_s,
    ask_send, ask_recv, row_send, row_recv, back_send, back_recv, total_send, total_recv, load_sem,
):
    me = lax.axis_index("space")
    points = target_ref.shape[1]
    width = mesh_ref.shape[1]
    rows = members * slots
    per = cap * members
    head_dim = width // HEADS
    group_heads = 256 // head_dim
    groups = HEADS // group_heads
    hs = group_heads * slots
    padded = pred_s.shape[0]

    loads = [
        pltpu.make_async_copy(src, dst, load_sem.at[i])
        for i, (src, dst) in enumerate(((x_hbm, x_s), (qw_hbm, qw_s), (kvw_hbm, kvw_s)))
    ]
    for load in loads:
        load.start()

    greet(shards, me)
    finish = exchange(shards, me, per, ask_ref, got_s, ask_send, ask_recv)
    got_s[part(me, per), :] = ask_ref[part(me, per), :]
    target_s[...] = jnp.zeros(target_s.shape, F32)
    target_s[0:fields, :] = target_ref[...]
    finish()
    select = selection(got_s[...], members, nodes)
    picked_s[...] = dot(select, mesh_ref[...], (1, 0)).astype(BF)
    finish = exchange(shards, me, per, picked_s, arrived_s, row_send, row_recv)
    arrived_s[part(me, per), :] = picked_s[part(me, per), :]
    loads[0].wait()
    loads[1].wait()
    for c in range(0, width, 256):
        q_s[:, c:c + 256] = dot(x_s[...], qw_s[:, c:c + 256], (1, 0)).astype(BF)
    order = order_matrix(rows, members, slots, cap)
    head_mask = (iota((hs, 256), 0) // slots == iota((hs, 256), 1) // head_dim).astype(F32)
    head_mask16 = head_mask.astype(BF)
    slot_ids = iota((slots, points), 0)
    named = (slot_ids == edge_ref[0:1, :]) | (slot_ids == edge_ref[1:2, :]) | (slot_ids == edge_ref[2:3, :])
    named = named.astype(F32)
    named = jnp.concatenate([named] * group_heads, axis=0) > 0.5
    loads[2].wait()
    finish()

    latent = dot(order, arrived_s[...], (1, 0)).astype(BF)
    for c in range(0, 2 * width, 512):
        kv_s[:, c:c + 512] = dot(latent, kvw_s[:, c:c + 512], (1, 0)).astype(BF)

    def blocks(values):
        return jnp.concatenate([values] * group_heads, axis=0) * head_mask16

    scale = 1.0 / math.sqrt(head_dim)

    def attend(e):
        rs, gs = part(e, slots), part(e, points)
        for k in range(groups):
            cs = slice(k * 256, (k + 1) * 256)
            keys = blocks(kv_s[rs, cs])
            values = blocks(kv_s[rs, width + k * 256:width + (k + 1) * 256])
            score = dot(keys, q_s[gs, cs], (1, 1)) * scale
            exponent = jnp.where(named, jnp.exp(score), 0.0)
            by_head = exponent.reshape(group_heads, slots, points)
            total = jnp.sum(by_head, axis=1, keepdims=True)
            weight = (by_head / total).reshape(hs, points)
            p_s[e, k] = weight
            att_s[cs, gs] = dot(values, weight.astype(BF), (0, 0)).astype(BF)

    def by_pairs(work):
        def step(i, carry):
            work(2 * i)
            work(2 * i + 1)
            return carry

        lax.fori_loop(0, members // 2, step, 0)

    by_pairs(attend)
    pred_s[0:fields, :] = dot(fw_ref[...], att_s[...], (1, 0))
    if padded > fields:
        pred_s[fields:padded, :] = jnp.zeros((padded - fields, members * points), F32)

    area = area_ref[...]
    almost_fair = 1.0 - (1.0 - FAIRNESS) / members
    spread_factor = almost_fair / (members * (members - 1))

    def judge(i, total):
        fs = part(i, 8)
        goal = target_s[fs, :]
        preds = [pred_s[fs, e * points:(e + 1) * points] for e in range(members)]
        slopes = []
        skill = jnp.zeros((8, points), F32)
        for e in range(members):
            u = preds[e] - goal
            v = u * u + SMOOTHING
            r = lax.rsqrt(v)
            skill += v * r
            slopes.append(u * r * (1.0 / members))
        spread = jnp.zeros((8, points), F32)
        pulls = [jnp.zeros((8, points), F32) for _ in range(members)]
        for a in range(members):
            for b in range(a + 1, members):
                u = preds[a] - preds[b]
                v = u * u + SMOOTHING
                r = lax.rsqrt(v)
                spread += v * r
                w = u * r
                pulls[a] = pulls[a] + w
                pulls[b] = pulls[b] - w
        pointwise = skill * (1.0 / members) - spread_factor * spread
        valid = iota((8, points), 0) + i * 8 < fields
        for e in range(members):
            dp_s[fs, e * points:(e + 1) * points] = (slopes[e] - spread_factor * pulls[e]) * area
        return total + jnp.where(valid, pointwise * area, 0.0)

    total_s[...] = lax.fori_loop(0, padded // 8, judge, jnp.zeros((8, points), F32))
    finish_total = exchange(shards, me, 8, total_s, totals_s, total_send, total_recv, whole=True)
    totals_s[part(me, 8), :] = total_s[...]

    dp = dp_s[0:fields, :].astype(BF)
    for k in range(groups):
        cs = slice(k * 256, (k + 1) * 256)
        da_s[cs, :] = dot(fw_ref[:, cs], dp, (0, 0)).astype(BF)

    def fold(product):
        kept = (product * head_mask).reshape(group_heads, slots, 256)
        return jnp.sum(kept, axis=0).astype(BF)

    def backward(e):
        rs, gs = part(e, slots), part(e, points)
        for k in range(groups):
            cs = slice(k * 256, (k + 1) * 256)
            vs = slice(width + k * 256, width + (k + 1) * 256)
            values = blocks(kv_s[rs, vs])
            weight = p_s[e, k]
            da = da_s[cs, gs]
            dw = dot(values, da, (1, 0))
            pull = (weight * dw).reshape(group_heads, slots, points)
            mean = jnp.sum(pull, axis=1, keepdims=True)
            ds = pull - weight.reshape(group_heads, slots, points) * mean
            ds = (ds.reshape(hs, points) * scale).astype(BF)
            sg_s[rs, cs] = fold(dot(ds, q_s[gs, cs], (1, 0)))
            sg_s[rs, vs] = fold(dot(weight.astype(BF), da, (1, 1)))

    by_pairs(backward)
    latent_grad = dot(sg_s[...], kvw_s[...], (1, 1)).astype(BF)
    grads_s[...] = dot(order, latent_grad, (0, 0)).astype(BF)
    finish = exchange(shards, me, per, grads_s, back_s, back_send, back_recv)
    back_s[part(me, per), :] = grads_s[part(me, per), :]
    finish_total()
    loss_ref[...] = jnp.full(loss_ref.shape, 1.0, F32) * (jnp.sum(totals_s[...]) / count)
    finish()
    out_ref[...] = dot(select, back_s[...], (0, 0)).astype(BF)


def decode(ask, mesh_rows, x, query_weight, kv_weight, field_weight, target, area, edge_slot, shards, members, cap):
    fields, points = target.shape
    width = mesh_rows.shape[1]
    nodes = mesh_rows.shape[0] // members
    slots = shards * cap
    rows = members * slots
    padded = -(-fields // 8) * 8
    group_heads = 256 * HEADS // width
    vmem = pl.BlockSpec(memory_space=pltpu.VMEM)
    hbm = pl.BlockSpec(memory_space=pl.ANY)
    sems = pltpu.SemaphoreType.DMA((shards,))
    count = float(fields * points * shards)
    return pl.pallas_call(
        functools.partial(decoder_kernel, shards, members, fields, slots, cap, nodes, count),
        out_shape=(
            jax.ShapeDtypeStruct(mesh_rows.shape, BF),
            jax.ShapeDtypeStruct((8, 128), F32),
        ),
        in_specs=[vmem] * 6 + [hbm] * 3,
        out_specs=(vmem, vmem),
        scratch_shapes=[
            pltpu.VMEM(x.shape, BF),
            pltpu.VMEM(query_weight.shape, BF),
            pltpu.VMEM(kv_weight.shape, BF),
            pltpu.VMEM(ask.shape, jnp.int32),
            pltpu.VMEM((rows, width), BF),
            pltpu.VMEM((rows, width), BF),
            pltpu.VMEM((rows, width), BF),
            pltpu.VMEM((rows, width), BF),
            pltpu.VMEM((8, points), F32),
            pltpu.VMEM((shards * 8, points), F32),
            pltpu.VMEM((members * points, width), BF),
            pltpu.VMEM((rows, 2 * width), BF),
            pltpu.VMEM((members, HEADS // group_heads, group_heads * slots, points), F32),
            pltpu.VMEM((width, members * points), BF),
            pltpu.VMEM((padded, points), F32),
            pltpu.VMEM((padded, members * points), F32),
            pltpu.VMEM((padded, members * points), F32),
            pltpu.VMEM((width, members * points), BF),
            pltpu.VMEM((rows, 2 * width), BF),
        ] + [sems] * 8 + [pltpu.SemaphoreType.DMA((3,))],
        compiler_params=pltpu.CompilerParams(
            collective_id=0, has_side_effects=True, vmem_limit_bytes=60 * 1024 * 1024
        ),
    )(ask, mesh_rows, field_weight, target, area, edge_slot, x, query_weight, kv_weight)


def local(
    grid_latent, mesh_latent, query_weight, kv_weight, field_weight, target, area_weight, request, edge_slot,
):
    members, points, width = grid_latent.shape
    nodes = mesh_latent.shape[1]
    shards = lax.axis_size("space")
    cap = request.shape[2]
    slots = shards * cap
    per = cap * members
    ask = jnp.broadcast_to(
        request.reshape(slots, 1, 1), (slots, members, 128)
    ).reshape(shards * per, 128)
    mesh_grad, loss = decode(
        ask, mesh_latent.reshape(members * nodes, width), grid_latent.reshape(members * points, width),
        query_weight, kv_weight, field_weight, target, area_weight.reshape(1, points), edge_slot,
        shards, members, cap,
    )
    mesh_grad = mesh_grad.reshape(members, nodes, width)
    mean_loss = loss[0, 0:1]
    return (mesh_grad, mean_loss)


def solution(mesh):
    placed = (
        P(None, ("groups", "space"), None),
        P(None, ("groups", "space"), None),
        P(),
        P(),
        P(),
        P(None, ("groups", "space")),
        P(("groups", "space")),
        P(("groups", "space"), None, None),
        P(None, ("groups", "space")),
    )
    return jax.shard_map(
        local,
        mesh=mesh,
        in_specs=placed,
        out_specs=(P(None, ("groups", "space"), None), P("groups")),
        check_vma=False,
    )
```

```python
import functools
import math

import jax
import jax.numpy as jnp
from jax import lax
from jax.experimental import pallas as pl
from jax.experimental.pallas import tpu as pltpu
from jax.sharding import PartitionSpec as P

HEADS = 16
SMOOTHING = 0.04
FAIRNESS = 0.95
PIECES = 2
BF = jnp.bfloat16
F32 = jnp.float32


def dot(a, b, dims):
    return lax.dot_general(a, b, ((dims[:1], dims[1:]), ((), ())), preferred_element_type=F32)


def iota(shape, dim):
    return lax.broadcasted_iota(jnp.int32, shape, dim)


def order_matrix(piece_members, slots, cap, column_part):
    rows, per = piece_members * slots, PIECES * cap * piece_members
    r, c = iota((rows, rows * PIECES), 0), iota((rows, rows * PIECES), 1)
    member, slot = r // slots, r % slots
    place = slot // cap * per + column_part * cap * piece_members + slot % cap * piece_members + member
    return (c == place).astype(F32).astype(BF)


def greet(shards, me):
    barrier = pltpu.get_barrier_semaphore()

    def tell(step, carry):
        partner = lax.rem(me + step, shards)
        pl.semaphore_signal(barrier, inc=1, device_id={"space": partner}, device_id_type=pl.DeviceIdType.MESH)
        return carry

    lax.fori_loop(1, shards, tell, 0)
    pl.semaphore_wait(barrier, shards - 1)


def part(index, size):
    return pl.ds(pl.multiple_of(index * size, size), size)


def exchange(shards, me, size, src, dst, send_sem, recv_sem, base=0, whole=False):
    def copy(partner, landing):
        return pltpu.make_async_remote_copy(
            src_ref=src if whole else src.at[part(partner, size)],
            dst_ref=dst.at[part(landing, size)],
            send_sem=send_sem.at[base + partner],
            recv_sem=recv_sem.at[base + landing],
            device_id={"space": partner},
            device_id_type=pl.DeviceIdType.MESH,
        )

    def start(step, carry):
        copy(lax.rem(me + step, shards), me).start()
        return carry

    def finish(step, carry):
        copy(lax.rem(me + step, shards), me).wait_send()
        sender = lax.rem(me + shards - step, shards)
        copy(sender, sender).wait_recv()
        return carry

    lax.fori_loop(1, shards, start, 0)
    return lambda: lax.fori_loop(1, shards, finish, 0)


def selection(got, piece_members, nodes):
    columns = piece_members * nodes
    lanes = min(128, columns)
    got = got[:, :lanes]
    member = iota(got.shape, 0) % piece_members
    lane = iota(got.shape, 1)
    parts = [
        (lane + c == member * nodes + got).astype(F32)
        for c in range(0, columns, lanes)
    ]
    return parts[0] if len(parts) == 1 else jnp.concatenate(parts, axis=1)


def decoder_kernel(
    shards, members, fields, slots, cap, nodes, count,
    ask_ref, mesh_ref, fw_ref, target_ref, area_ref, edge_ref, x_hbm, qw_hbm, kvw_hbm,
    out_ref, loss_ref,
    x_s, qw_s, kvw_s, got_s, picked_s, arrived_s, grads_s, back_s, total_s, totals_s,
    q_s, kv_s, p_s, att_s, target_s, pred_s, dp_s, da_s, sg_s,
    ask_send, ask_recv, row_send, row_recv, back_send, back_recv, total_send, total_recv, load_sem,
):
    me = lax.axis_index("space")
    points = target_ref.shape[1]
    width = mesh_ref.shape[1]
    rows = members * slots
    per = cap * members
    head_dim = width // HEADS
    group_heads = 256 // head_dim
    groups = HEADS // group_heads
    hs = group_heads * slots
    padded = pred_s.shape[0]

    loads = [
        pltpu.make_async_copy(src, dst, load_sem.at[i])
        for i, (src, dst) in enumerate(((x_hbm, x_s), (qw_hbm, qw_s), (kvw_hbm, kvw_s)))
    ]
    for load in loads:
        load.start()

    greet(shards, me)
    finish = exchange(shards, me, per, ask_ref, got_s, ask_send, ask_recv)
    got_s[part(me, per), :] = ask_ref[part(me, per), :]
    target_s[...] = jnp.zeros(target_s.shape, F32)
    target_s[0:fields, :] = target_ref[...]
    finish()
    piece_members = members // PIECES
    piece_rows = piece_members * nodes
    wire_rows = shards * per
    wide = width // PIECES
    select = selection(got_s[...], piece_members, nodes)
    column_part = iota(select.shape, 0) % per // (cap * piece_members)
    selects = [jnp.where(column_part == p, select, 0.0).astype(BF) for p in range(PIECES)]
    finish_rows = []
    for h in range(PIECES):
        ws = slice(h * wire_rows, (h + 1) * wire_rows)
        picked = jnp.zeros((wire_rows, wide), F32)
        for p in range(PIECES):
            source = mesh_ref[h * piece_rows:(h + 1) * piece_rows, p * wide:(p + 1) * wide]
            picked += dot(selects[p], source, (1, 0))
        picked_s[ws, :] = picked.astype(BF)
        source, landing = picked_s.at[ws], arrived_s.at[ws]
        finish_rows.append(exchange(
            shards, me, per, source, landing, row_send, row_recv, base=h * shards
        ))
        own = part(me + h * shards, per)
        arrived_s[own, :] = picked_s[own, :]
    loads[0].wait()
    loads[1].wait()
    for c in range(0, width, 256):
        q_s[:, c:c + 256] = dot(x_s[...], qw_s[:, c:c + 256], (1, 0)).astype(BF)
    orders = [order_matrix(piece_members, slots, cap, p) for p in range(PIECES)]
    head_mask = (iota((hs, 256), 0) // slots == iota((hs, 256), 1) // head_dim).astype(F32)
    head_mask16 = head_mask.astype(BF)
    slot_ids = iota((slots, points), 0)
    named = (slot_ids == edge_ref[0:1, :]) | (slot_ids == edge_ref[1:2, :]) | (slot_ids == edge_ref[2:3, :])
    named = named.astype(F32)
    named = jnp.concatenate([named] * group_heads, axis=0) > 0.5
    loads[2].wait()

    def blocks(values):
        return jnp.concatenate([values] * group_heads, axis=0) * head_mask16

    scale = 1.0 / math.sqrt(head_dim)

    def attend(e):
        rs, gs = part(e, slots), part(e, points)
        for k in range(groups):
            cs = slice(k * 256, (k + 1) * 256)
            keys = blocks(kv_s[rs, cs])
            values = blocks(kv_s[rs, width + k * 256:width + (k + 1) * 256])
            score = dot(keys, q_s[gs, cs], (1, 1)) * scale
            exponent = jnp.where(named, jnp.exp(score), 0.0)
            by_head = exponent.reshape(group_heads, slots, points)
            total = jnp.sum(by_head, axis=1, keepdims=True)
            weight = (by_head / total).reshape(hs, points)
            p_s[e, k] = weight
            att_s[cs, gs] = dot(values, weight.astype(BF), (0, 0)).astype(BF)

    def by_pairs(work, h):
        first = h * piece_members
        for e in range(0, piece_members % 2):
            work(first + e)

        def step(i, carry):
            work(first + piece_members % 2 + 2 * i)
            work(first + piece_members % 2 + 2 * i + 1)
            return carry

        lax.fori_loop(0, piece_members // 2, step, 0)

    kv_rows = piece_members * slots
    for h in range(PIECES):
        finish_rows[h]()
        arrived = arrived_s[h * wire_rows:(h + 1) * wire_rows, :]
        latent = jnp.concatenate(
            [dot(orders[p], arrived, (1, 0)).astype(BF) for p in range(PIECES)], axis=1
        )
        for c in range(0, 2 * width, 512):
            kv_s[h * kv_rows:(h + 1) * kv_rows, c:c + 512] = dot(
                latent, kvw_s[:, c:c + 512], (1, 0)
            ).astype(BF)
        by_pairs(attend, h)
    pred_s[0:fields, :] = dot(fw_ref[...], att_s[...], (1, 0))
    if padded > fields:
        pred_s[fields:padded, :] = jnp.zeros((padded - fields, members * points), F32)

    area = area_ref[...]
    almost_fair = 1.0 - (1.0 - FAIRNESS) / members
    spread_factor = almost_fair / (members * (members - 1))

    def judge(i, total):
        fs = part(i, 8)
        goal = target_s[fs, :]
        preds = [pred_s[fs, e * points:(e + 1) * points] for e in range(members)]
        slopes = []
        skill = jnp.zeros((8, points), F32)
        for e in range(members):
            u = preds[e] - goal
            v = u * u + SMOOTHING
            r = lax.rsqrt(v)
            skill += v * r
            slopes.append(u * r * (1.0 / members))
        spread = jnp.zeros((8, points), F32)
        pulls = [jnp.zeros((8, points), F32) for _ in range(members)]
        for a in range(members):
            for b in range(a + 1, members):
                u = preds[a] - preds[b]
                v = u * u + SMOOTHING
                r = lax.rsqrt(v)
                spread += v * r
                w = u * r
                pulls[a] = pulls[a] + w
                pulls[b] = pulls[b] - w
        pointwise = skill * (1.0 / members) - spread_factor * spread
        valid = iota((8, points), 0) + i * 8 < fields
        for e in range(members):
            dp_s[fs, e * points:(e + 1) * points] = (slopes[e] - spread_factor * pulls[e]) * area
        return total + jnp.where(valid, pointwise * area, 0.0)

    total_s[...] = lax.fori_loop(0, padded // 8, judge, jnp.zeros((8, points), F32))
    finish_total = exchange(shards, me, 8, total_s, totals_s, total_send, total_recv, whole=True)
    totals_s[part(me, 8), :] = total_s[...]

    dp = dp_s[0:fields, :].astype(BF)
    for k in range(groups):
        cs = slice(k * 256, (k + 1) * 256)
        da_s[cs, :] = dot(fw_ref[:, cs], dp, (0, 0)).astype(BF)

    def fold(product):
        kept = (product * head_mask).reshape(group_heads, slots, 256)
        return jnp.sum(kept, axis=0).astype(BF)

    def backward(e):
        rs, gs = part(e, slots), part(e, points)
        for k in range(groups):
            cs = slice(k * 256, (k + 1) * 256)
            vs = slice(width + k * 256, width + (k + 1) * 256)
            values = blocks(kv_s[rs, vs])
            weight = p_s[e, k]
            da = da_s[cs, gs]
            dw = dot(values, da, (1, 0))
            pull = (weight * dw).reshape(group_heads, slots, points)
            mean = jnp.sum(pull, axis=1, keepdims=True)
            ds = pull - weight.reshape(group_heads, slots, points) * mean
            ds = (ds.reshape(hs, points) * scale).astype(BF)
            sg_s[rs, cs] = fold(dot(ds, q_s[gs, cs], (1, 0)))
            sg_s[rs, vs] = fold(dot(weight.astype(BF), da, (1, 1)))

    finish_back = []
    for h in range(PIECES):
        by_pairs(backward, h)
        ws = slice(h * wire_rows, (h + 1) * wire_rows)
        latent_grad = dot(sg_s[h * kv_rows:(h + 1) * kv_rows, :], kvw_s[...], (1, 1)).astype(BF)
        sent = jnp.zeros((wire_rows, wide), F32)
        for p in range(PIECES):
            sent += dot(orders[p], latent_grad[:, p * wide:(p + 1) * wide], (0, 0))
        grads_s[ws, :] = sent.astype(BF)
        finish_back.append(exchange(
            shards, me, per, grads_s.at[ws], back_s.at[ws], back_send, back_recv, base=h * shards
        ))
        own = part(me + h * shards, per)
        back_s[own, :] = grads_s[own, :]
    finish_total()
    loss_ref[...] = jnp.full(loss_ref.shape, 1.0, F32) * (jnp.sum(totals_s[...]) / count)
    for h in range(PIECES):
        finish_back[h]()
        back = back_s[h * wire_rows:(h + 1) * wire_rows, :]
        for p in range(PIECES):
            out_ref[h * piece_rows:(h + 1) * piece_rows, p * wide:(p + 1) * wide] = dot(
                selects[p], back, (0, 0)
            ).astype(BF)


def decode(ask, mesh_rows, x, query_weight, kv_weight, field_weight, target, area, edge_slot, shards, members, cap):
    fields, points = target.shape
    width = mesh_rows.shape[1]
    nodes = mesh_rows.shape[0] // members
    slots = shards * cap
    rows = members * slots
    padded = -(-fields // 8) * 8
    group_heads = 256 * HEADS // width
    vmem = pl.BlockSpec(memory_space=pltpu.VMEM)
    hbm = pl.BlockSpec(memory_space=pl.ANY)
    sems = pltpu.SemaphoreType.DMA((shards,))
    piece_sems = pltpu.SemaphoreType.DMA((PIECES * shards,))
    count = float(fields * points * shards)
    return pl.pallas_call(
        functools.partial(decoder_kernel, shards, members, fields, slots, cap, nodes, count),
        out_shape=(
            jax.ShapeDtypeStruct(mesh_rows.shape, BF),
            jax.ShapeDtypeStruct((8, 128), F32),
        ),
        in_specs=[vmem] * 6 + [hbm] * 3,
        out_specs=(vmem, vmem),
        scratch_shapes=[
            pltpu.VMEM(x.shape, BF),
            pltpu.VMEM(query_weight.shape, BF),
            pltpu.VMEM(kv_weight.shape, BF),
            pltpu.VMEM(ask.shape, jnp.int32),
            pltpu.VMEM((PIECES * rows, width // PIECES), BF),
            pltpu.VMEM((PIECES * rows, width // PIECES), BF),
            pltpu.VMEM((PIECES * rows, width // PIECES), BF),
            pltpu.VMEM((PIECES * rows, width // PIECES), BF),
            pltpu.VMEM((8, points), F32),
            pltpu.VMEM((shards * 8, points), F32),
            pltpu.VMEM((members * points, width), BF),
            pltpu.VMEM((rows, 2 * width), BF),
            pltpu.VMEM((members, HEADS // group_heads, group_heads * slots, points), F32),
            pltpu.VMEM((width, members * points), BF),
            pltpu.VMEM((padded, points), F32),
            pltpu.VMEM((padded, members * points), F32),
            pltpu.VMEM((padded, members * points), F32),
            pltpu.VMEM((width, members * points), BF),
            pltpu.VMEM((rows, 2 * width), BF),
        ] + [sems] * 2 + [piece_sems] * 4 + [sems] * 2 + [pltpu.SemaphoreType.DMA((3,))],
        compiler_params=pltpu.CompilerParams(
            collective_id=0, has_side_effects=True, vmem_limit_bytes=60 * 1024 * 1024
        ),
    )(ask, mesh_rows, field_weight, target, area, edge_slot, x, query_weight, kv_weight)


def local(
    grid_latent, mesh_latent, query_weight, kv_weight, field_weight, target, area_weight, request, edge_slot,
):
    members, points, width = grid_latent.shape
    nodes = mesh_latent.shape[1]
    shards = lax.axis_size("space")
    cap = request.shape[2]
    slots = shards * cap
    per = cap * members
    ask = jnp.broadcast_to(
        request.reshape(shards, 1, cap, 1, 1), (shards, PIECES, cap, members // PIECES, 128)
    ).reshape(shards * per, 128)
    mesh_grad, loss = decode(
        ask, mesh_latent.reshape(members * nodes, width), grid_latent.reshape(members * points, width),
        query_weight, kv_weight, field_weight, target, area_weight.reshape(1, points), edge_slot,
        shards, members, cap,
    )
    mesh_grad = mesh_grad.reshape(members, nodes, width)
    mean_loss = loss[0, 0:1]
    return (mesh_grad, mean_loss)


def solution(mesh):
    placed = (
        P(None, ("groups", "space"), None),
        P(None, ("groups", "space"), None),
        P(),
        P(),
        P(),
        P(None, ("groups", "space")),
        P(("groups", "space")),
        P(("groups", "space"), None, None),
        P(None, ("groups", "space")),
    )
    return jax.shard_map(
        local,
        mesh=mesh,
        in_specs=placed,
        out_specs=(P(None, ("groups", "space"), None), P("groups")),
        check_vma=False,
    )
```

```python
import functools
import math

import jax
import jax.numpy as jnp
from jax import lax
from jax.experimental import pallas as pl
from jax.experimental.pallas import tpu as pltpu
from jax.sharding import PartitionSpec as P

HEADS = 16
SMOOTHING = 0.04
FAIRNESS = 0.95
PIECES = 4
BF = jnp.bfloat16
F32 = jnp.float32


def dot(a, b, dims):
    return lax.dot_general(a, b, ((dims[:1], dims[1:]), ((), ())), preferred_element_type=F32)


def iota(shape, dim):
    return lax.broadcasted_iota(jnp.int32, shape, dim)


def order_matrix(piece_members, slots, cap, column_part):
    rows, per = piece_members * slots, PIECES * cap * piece_members
    r, c = iota((rows, rows * PIECES), 0), iota((rows, rows * PIECES), 1)
    member, slot = r // slots, r % slots
    place = slot // cap * per + column_part * cap * piece_members + slot % cap * piece_members + member
    return (c == place).astype(F32).astype(BF)


def greet(shards, me):
    barrier = pltpu.get_barrier_semaphore()

    def tell(step, carry):
        partner = lax.rem(me + step, shards)
        pl.semaphore_signal(barrier, inc=1, device_id={"space": partner}, device_id_type=pl.DeviceIdType.MESH)
        return carry

    lax.fori_loop(1, shards, tell, 0)
    pl.semaphore_wait(barrier, shards - 1)


def part(index, size):
    return pl.ds(pl.multiple_of(index * size, size), size)


def exchange(shards, me, size, src, dst, send_sem, recv_sem, base=0, whole=False):
    def copy(partner, landing):
        return pltpu.make_async_remote_copy(
            src_ref=src if whole else src.at[part(partner, size)],
            dst_ref=dst.at[part(landing, size)],
            send_sem=send_sem.at[base + partner],
            recv_sem=recv_sem.at[base + landing],
            device_id={"space": partner},
            device_id_type=pl.DeviceIdType.MESH,
        )

    def start(step, carry):
        copy(lax.rem(me + step, shards), me).start()
        return carry

    def finish(step, carry):
        copy(lax.rem(me + step, shards), me).wait_send()
        sender = lax.rem(me + shards - step, shards)
        copy(sender, sender).wait_recv()
        return carry

    lax.fori_loop(1, shards, start, 0)
    return lambda: lax.fori_loop(1, shards, finish, 0)


def selection(got, piece_members, nodes):
    columns = piece_members * nodes
    lanes = min(128, columns)
    got = got[:, :lanes]
    member = iota(got.shape, 0) % piece_members
    lane = iota(got.shape, 1)
    parts = [
        (lane + c == member * nodes + got).astype(F32)
        for c in range(0, columns, lanes)
    ]
    return parts[0] if len(parts) == 1 else jnp.concatenate(parts, axis=1)


def decoder_kernel(
    shards, members, fields, slots, cap, nodes, count,
    ask_ref, mesh_ref, fw_ref, target_ref, area_ref, edge_ref, x_hbm, qw_hbm, kvw_hbm,
    out_ref, loss_ref,
    x_s, qw_s, kvw_s, got_s, picked_s, arrived_s, grads_s, back_s, total_s, totals_s,
    q_s, kv_s, p_s, att_s, target_s, pred_s, dp_s, da_s, sg_s,
    ask_send, ask_recv, row_send, row_recv, back_send, back_recv, total_send, total_recv, load_sem,
):
    me = lax.axis_index("space")
    points = target_ref.shape[1]
    width = mesh_ref.shape[1]
    rows = members * slots
    per = cap * members
    head_dim = width // HEADS
    group_heads = 256 // head_dim
    groups = HEADS // group_heads
    hs = group_heads * slots
    padded = pred_s.shape[0]

    loads = [
        pltpu.make_async_copy(src, dst, load_sem.at[i])
        for i, (src, dst) in enumerate(((x_hbm, x_s), (qw_hbm, qw_s), (kvw_hbm, kvw_s)))
    ]
    for load in loads:
        load.start()

    greet(shards, me)
    finish = exchange(shards, me, per, ask_ref, got_s, ask_send, ask_recv)
    got_s[part(me, per), :] = ask_ref[part(me, per), :]
    target_s[...] = jnp.zeros(target_s.shape, F32)
    target_s[0:fields, :] = target_ref[...]
    finish()
    piece_members = members // PIECES
    piece_rows = piece_members * nodes
    wire_rows = shards * per
    wide = width // PIECES
    select = selection(got_s[...], piece_members, nodes)
    column_part = iota(select.shape, 0) % per // (cap * piece_members)
    selects = [jnp.where(column_part == p, select, 0.0).astype(BF) for p in range(PIECES)]
    finish_rows = []
    for h in range(PIECES):
        ws = slice(h * wire_rows, (h + 1) * wire_rows)
        picked = jnp.zeros((wire_rows, wide), F32)
        for p in range(PIECES):
            source = mesh_ref[h * piece_rows:(h + 1) * piece_rows, p * wide:(p + 1) * wide]
            picked += dot(selects[p], source, (1, 0))
        picked_s[ws, :] = picked.astype(BF)
        source, landing = picked_s.at[ws], arrived_s.at[ws]
        finish_rows.append(exchange(
            shards, me, per, source, landing, row_send, row_recv, base=h * shards
        ))
        own = part(me + h * shards, per)
        arrived_s[own, :] = picked_s[own, :]
    loads[0].wait()
    loads[1].wait()
    for c in range(0, width, 256):
        q_s[:, c:c + 256] = dot(x_s[...], qw_s[:, c:c + 256], (1, 0)).astype(BF)
    orders = [order_matrix(piece_members, slots, cap, p) for p in range(PIECES)]
    head_mask = (iota((hs, 256), 0) // slots == iota((hs, 256), 1) // head_dim).astype(F32)
    head_mask16 = head_mask.astype(BF)
    slot_ids = iota((slots, points), 0)
    named = (slot_ids == edge_ref[0:1, :]) | (slot_ids == edge_ref[1:2, :]) | (slot_ids == edge_ref[2:3, :])
    named = named.astype(F32)
    named = jnp.concatenate([named] * group_heads, axis=0) > 0.5
    loads[2].wait()

    def blocks(values):
        return jnp.concatenate([values] * group_heads, axis=0) * head_mask16

    scale = 1.0 / math.sqrt(head_dim)

    def attend(e):
        rs, gs = part(e, slots), part(e, points)
        for k in range(groups):
            cs = slice(k * 256, (k + 1) * 256)
            keys = blocks(kv_s[rs, cs])
            values = blocks(kv_s[rs, width + k * 256:width + (k + 1) * 256])
            score = dot(keys, q_s[gs, cs], (1, 1)) * scale
            exponent = jnp.where(named, jnp.exp(score), 0.0)
            by_head = exponent.reshape(group_heads, slots, points)
            total = jnp.sum(by_head, axis=1, keepdims=True)
            weight = (by_head / total).reshape(hs, points)
            p_s[e, k] = weight
            att_s[cs, gs] = dot(values, weight.astype(BF), (0, 0)).astype(BF)

    def by_pairs(work, h):
        first = h * piece_members
        for e in range(0, piece_members % 2):
            work(first + e)

        def step(i, carry):
            work(first + piece_members % 2 + 2 * i)
            work(first + piece_members % 2 + 2 * i + 1)
            return carry

        lax.fori_loop(0, piece_members // 2, step, 0)

    kv_rows = piece_members * slots
    for h in range(PIECES):
        finish_rows[h]()
        arrived = arrived_s[h * wire_rows:(h + 1) * wire_rows, :]
        latent = jnp.concatenate(
            [dot(orders[p], arrived, (1, 0)).astype(BF) for p in range(PIECES)], axis=1
        )
        for c in range(0, 2 * width, 512):
            kv_s[h * kv_rows:(h + 1) * kv_rows, c:c + 512] = dot(
                latent, kvw_s[:, c:c + 512], (1, 0)
            ).astype(BF)
        by_pairs(attend, h)
    pred_s[0:fields, :] = dot(fw_ref[...], att_s[...], (1, 0))
    if padded > fields:
        pred_s[fields:padded, :] = jnp.zeros((padded - fields, members * points), F32)

    area = area_ref[...]
    almost_fair = 1.0 - (1.0 - FAIRNESS) / members
    spread_factor = almost_fair / (members * (members - 1))

    def judge(i, total):
        fs = part(i, 8)
        goal = target_s[fs, :]
        preds = [pred_s[fs, e * points:(e + 1) * points] for e in range(members)]
        slopes = []
        skill = jnp.zeros((8, points), F32)
        for e in range(members):
            u = preds[e] - goal
            v = u * u + SMOOTHING
            r = lax.rsqrt(v)
            skill += v * r
            slopes.append(u * r * (1.0 / members))
        spread = jnp.zeros((8, points), F32)
        pulls = [jnp.zeros((8, points), F32) for _ in range(members)]
        for a in range(members):
            for b in range(a + 1, members):
                u = preds[a] - preds[b]
                v = u * u + SMOOTHING
                r = lax.rsqrt(v)
                spread += v * r
                w = u * r
                pulls[a] = pulls[a] + w
                pulls[b] = pulls[b] - w
        pointwise = skill * (1.0 / members) - spread_factor * spread
        valid = iota((8, points), 0) + i * 8 < fields
        for e in range(members):
            dp_s[fs, e * points:(e + 1) * points] = (slopes[e] - spread_factor * pulls[e]) * area
        return total + jnp.where(valid, pointwise * area, 0.0)

    total_s[...] = lax.fori_loop(0, padded // 8, judge, jnp.zeros((8, points), F32))
    finish_total = exchange(shards, me, 8, total_s, totals_s, total_send, total_recv, whole=True)
    totals_s[part(me, 8), :] = total_s[...]

    dp = dp_s[0:fields, :].astype(BF)
    for k in range(groups):
        cs = slice(k * 256, (k + 1) * 256)
        da_s[cs, :] = dot(fw_ref[:, cs], dp, (0, 0)).astype(BF)

    def fold(product):
        kept = (product * head_mask).reshape(group_heads, slots, 256)
        return jnp.sum(kept, axis=0).astype(BF)

    def backward(e):
        rs, gs = part(e, slots), part(e, points)
        for k in range(groups):
            cs = slice(k * 256, (k + 1) * 256)
            vs = slice(width + k * 256, width + (k + 1) * 256)
            values = blocks(kv_s[rs, vs])
            weight = p_s[e, k]
            da = da_s[cs, gs]
            dw = dot(values, da, (1, 0))
            pull = (weight * dw).reshape(group_heads, slots, points)
            mean = jnp.sum(pull, axis=1, keepdims=True)
            ds = pull - weight.reshape(group_heads, slots, points) * mean
            ds = (ds.reshape(hs, points) * scale).astype(BF)
            sg_s[rs, cs] = fold(dot(ds, q_s[gs, cs], (1, 0)))
            sg_s[rs, vs] = fold(dot(weight.astype(BF), da, (1, 1)))

    finish_back = []
    for h in range(PIECES):
        by_pairs(backward, h)
        ws = slice(h * wire_rows, (h + 1) * wire_rows)
        latent_grad = dot(sg_s[h * kv_rows:(h + 1) * kv_rows, :], kvw_s[...], (1, 1)).astype(BF)
        sent = jnp.zeros((wire_rows, wide), F32)
        for p in range(PIECES):
            sent += dot(orders[p], latent_grad[:, p * wide:(p + 1) * wide], (0, 0))
        grads_s[ws, :] = sent.astype(BF)
        finish_back.append(exchange(
            shards, me, per, grads_s.at[ws], back_s.at[ws], back_send, back_recv, base=h * shards
        ))
        own = part(me + h * shards, per)
        back_s[own, :] = grads_s[own, :]
    finish_total()
    loss_ref[...] = jnp.full(loss_ref.shape, 1.0, F32) * (jnp.sum(totals_s[...]) / count)
    for h in range(PIECES):
        finish_back[h]()
        back = back_s[h * wire_rows:(h + 1) * wire_rows, :]
        for p in range(PIECES):
            out_ref[h * piece_rows:(h + 1) * piece_rows, p * wide:(p + 1) * wide] = dot(
                selects[p], back, (0, 0)
            ).astype(BF)


def decode(ask, mesh_rows, x, query_weight, kv_weight, field_weight, target, area, edge_slot, shards, members, cap):
    fields, points = target.shape
    width = mesh_rows.shape[1]
    nodes = mesh_rows.shape[0] // members
    slots = shards * cap
    rows = members * slots
    padded = -(-fields // 8) * 8
    group_heads = 256 * HEADS // width
    vmem = pl.BlockSpec(memory_space=pltpu.VMEM)
    hbm = pl.BlockSpec(memory_space=pl.ANY)
    sems = pltpu.SemaphoreType.DMA((shards,))
    piece_sems = pltpu.SemaphoreType.DMA((PIECES * shards,))
    count = float(fields * points * shards)
    return pl.pallas_call(
        functools.partial(decoder_kernel, shards, members, fields, slots, cap, nodes, count),
        out_shape=(
            jax.ShapeDtypeStruct(mesh_rows.shape, BF),
            jax.ShapeDtypeStruct((8, 128), F32),
        ),
        in_specs=[vmem] * 6 + [hbm] * 3,
        out_specs=(vmem, vmem),
        scratch_shapes=[
            pltpu.VMEM(x.shape, BF),
            pltpu.VMEM(query_weight.shape, BF),
            pltpu.VMEM(kv_weight.shape, BF),
            pltpu.VMEM(ask.shape, jnp.int32),
            pltpu.VMEM((PIECES * rows, width // PIECES), BF),
            pltpu.VMEM((PIECES * rows, width // PIECES), BF),
            pltpu.VMEM((PIECES * rows, width // PIECES), BF),
            pltpu.VMEM((PIECES * rows, width // PIECES), BF),
            pltpu.VMEM((8, points), F32),
            pltpu.VMEM((shards * 8, points), F32),
            pltpu.VMEM((members * points, width), BF),
            pltpu.VMEM((rows, 2 * width), BF),
            pltpu.VMEM((members, HEADS // group_heads, group_heads * slots, points), F32),
            pltpu.VMEM((width, members * points), BF),
            pltpu.VMEM((padded, points), F32),
            pltpu.VMEM((padded, members * points), F32),
            pltpu.VMEM((padded, members * points), F32),
            pltpu.VMEM((width, members * points), BF),
            pltpu.VMEM((rows, 2 * width), BF),
        ] + [sems] * 2 + [piece_sems] * 4 + [sems] * 2 + [pltpu.SemaphoreType.DMA((3,))],
        compiler_params=pltpu.CompilerParams(
            collective_id=0, has_side_effects=True, vmem_limit_bytes=60 * 1024 * 1024
        ),
    )(ask, mesh_rows, field_weight, target, area, edge_slot, x, query_weight, kv_weight)


def local(
    grid_latent, mesh_latent, query_weight, kv_weight, field_weight, target, area_weight, request, edge_slot,
):
    members, points, width = grid_latent.shape
    nodes = mesh_latent.shape[1]
    shards = lax.axis_size("space")
    cap = request.shape[2]
    slots = shards * cap
    per = cap * members
    ask = jnp.broadcast_to(
        request.reshape(shards, 1, cap, 1, 1), (shards, PIECES, cap, members // PIECES, 128)
    ).reshape(shards * per, 128)
    mesh_grad, loss = decode(
        ask, mesh_latent.reshape(members * nodes, width), grid_latent.reshape(members * points, width),
        query_weight, kv_weight, field_weight, target, area_weight.reshape(1, points), edge_slot,
        shards, members, cap,
    )
    mesh_grad = mesh_grad.reshape(members, nodes, width)
    mean_loss = loss[0, 0:1]
    return (mesh_grad, mean_loss)


def solution(mesh):
    placed = (
        P(None, ("groups", "space"), None),
        P(None, ("groups", "space"), None),
        P(),
        P(),
        P(),
        P(None, ("groups", "space")),
        P(("groups", "space")),
        P(("groups", "space"), None, None),
        P(None, ("groups", "space")),
    )
    return jax.shard_map(
        local,
        mesh=mesh,
        in_specs=placed,
        out_specs=(P(None, ("groups", "space"), None), P("groups")),
        check_vma=False,
    )
```

```python
import functools
import math

import jax
import jax.numpy as jnp
from jax import lax
from jax.experimental import pallas as pl
from jax.experimental.pallas import tpu as pltpu
from jax.sharding import PartitionSpec as P

HEADS = 16
SMOOTHING = 0.04
FAIRNESS = 0.95
PIECES = 2
BF = jnp.bfloat16
F32 = jnp.float32


def dot(a, b, dims):
    return lax.dot_general(a, b, ((dims[:1], dims[1:]), ((), ())), preferred_element_type=F32)


def iota(shape, dim):
    return lax.broadcasted_iota(jnp.int32, shape, dim)


def order_matrix(piece_members, slots, cap, column_part):
    rows, per = piece_members * slots, PIECES * cap * piece_members
    r, c = iota((rows, rows * PIECES), 0), iota((rows, rows * PIECES), 1)
    member, slot = r // slots, r % slots
    place = slot // cap * per + column_part * cap * piece_members + slot % cap * piece_members + member
    return (c == place).astype(F32).astype(BF)


def greet(shards, me):
    barrier = pltpu.get_barrier_semaphore()

    def tell(step, carry):
        partner = lax.rem(me + step, shards)
        pl.semaphore_signal(barrier, inc=1, device_id={"space": partner}, device_id_type=pl.DeviceIdType.MESH)
        return carry

    lax.fori_loop(1, shards, tell, 0)
    pl.semaphore_wait(barrier, shards - 1)


def part(index, size):
    return pl.ds(pl.multiple_of(index * size, size), size)


def exchange(shards, me, size, src, dst, send_sem, recv_sem, base=0, whole=False):
    def copy(partner, landing):
        return pltpu.make_async_remote_copy(
            src_ref=src if whole else src.at[part(partner, size)],
            dst_ref=dst.at[part(landing, size)],
            send_sem=send_sem.at[base + partner],
            recv_sem=recv_sem.at[base + landing],
            device_id={"space": partner},
            device_id_type=pl.DeviceIdType.MESH,
        )

    def start(step, carry):
        copy(lax.rem(me + step, shards), me).start()
        return carry

    def finish(step, carry):
        copy(lax.rem(me + step, shards), me).wait_send()
        sender = lax.rem(me + shards - step, shards)
        copy(sender, sender).wait_recv()
        return carry

    lax.fori_loop(1, shards, start, 0)
    return lambda: lax.fori_loop(1, shards, finish, 0)


def selection(got, piece_members, nodes):
    columns = piece_members * nodes
    lanes = min(128, columns)
    got = got[:, :lanes]
    member = iota(got.shape, 0) % piece_members
    lane = iota(got.shape, 1)
    parts = [
        (lane + c == member * nodes + got).astype(F32)
        for c in range(0, columns, lanes)
    ]
    return parts[0] if len(parts) == 1 else jnp.concatenate(parts, axis=1)


def decoder_kernel(
    shards, members, fields, slots, cap, nodes, count,
    ask_ref, mesh_ref, fw_ref, target_ref, area_ref, edge_ref, x_hbm, qw_hbm, kvw_hbm,
    out_ref, loss_ref,
    x_s, qw_s, kvw_s, got_s, picked_s, arrived_s, grads_s, back_s, total_s, totals_s,
    q_s, kv_s, p_s, att_s, target_s, pred_s, dp_s, da_s, sg_s,
    ask_send, ask_recv, row_send, row_recv, back_send, back_recv, total_send, total_recv, load_sem,
):
    me = lax.axis_index("space")
    points = target_ref.shape[1]
    width = mesh_ref.shape[1]
    rows = members * slots
    per = cap * members
    head_dim = width // HEADS
    group_heads = 256 // head_dim
    groups = HEADS // group_heads
    hs = group_heads * slots
    padded = pred_s.shape[0]

    loads = [
        pltpu.make_async_copy(src, dst, load_sem.at[i])
        for i, (src, dst) in enumerate(((x_hbm, x_s), (qw_hbm, qw_s), (kvw_hbm, kvw_s)))
    ]
    for load in loads:
        load.start()

    greet(shards, me)
    finish = exchange(shards, me, per, ask_ref, got_s, ask_send, ask_recv)
    got_s[part(me, per), :] = ask_ref[part(me, per), :]
    target_s[...] = jnp.zeros(target_s.shape, F32)
    target_s[0:fields, :] = target_ref[...]
    finish()
    piece_members = members // PIECES
    piece_rows = piece_members * nodes
    wire_rows = shards * per
    wide = width // PIECES
    select = selection(got_s[...], piece_members, nodes)
    column_part = iota(select.shape, 0) % per // (cap * piece_members)
    selects = [jnp.where(column_part == p, select, 0.0).astype(BF) for p in range(PIECES)]
    finish_rows = []
    for h in range(PIECES):
        ws = slice(h * wire_rows, (h + 1) * wire_rows)
        picked = jnp.zeros((wire_rows, wide), F32)
        for p in range(PIECES):
            source = mesh_ref[h * piece_rows:(h + 1) * piece_rows, p * wide:(p + 1) * wide]
            picked += dot(selects[p], source, (1, 0))
        picked_s[ws, :] = picked.astype(BF)
        source, landing = picked_s.at[ws], arrived_s.at[ws]
        finish_rows.append(exchange(
            shards, me, per, source, landing, row_send, row_recv, base=h * shards
        ))
        own = part(me + h * shards, per)
        arrived_s[own, :] = picked_s[own, :]
    loads[0].wait()
    loads[1].wait()
    for c in range(0, width, 256):
        q_s[:, c:c + 256] = dot(x_s[...], qw_s[:, c:c + 256], (1, 0)).astype(BF)
    orders = [order_matrix(piece_members, slots, cap, p) for p in range(PIECES)]
    head_mask = (iota((hs, 256), 0) // slots == iota((hs, 256), 1) // head_dim).astype(F32)
    head_mask16 = head_mask.astype(BF)
    slot_ids = iota((slots, points), 0)
    named = (slot_ids == edge_ref[0:1, :]) | (slot_ids == edge_ref[1:2, :]) | (slot_ids == edge_ref[2:3, :])
    named = named.astype(F32)
    named = jnp.concatenate([named] * group_heads, axis=0) > 0.5
    loads[2].wait()

    def blocks(values):
        return jnp.concatenate([values] * group_heads, axis=0) * head_mask16

    scale = 1.0 / math.sqrt(head_dim)

    def attend(e):
        rs, gs = part(e, slots), part(e, points)
        for k in range(groups):
            cs = slice(k * 256, (k + 1) * 256)
            keys = blocks(kv_s[rs, cs])
            values = blocks(kv_s[rs, width + k * 256:width + (k + 1) * 256])
            score = dot(keys, q_s[gs, cs], (1, 1)) * scale
            exponent = jnp.where(named, jnp.exp(score), 0.0)
            by_head = exponent.reshape(group_heads, slots, points)
            total = jnp.sum(by_head, axis=1, keepdims=True)
            weight = (by_head / total).reshape(hs, points)
            p_s[e, k] = weight
            att_s[cs, gs] = dot(values, weight.astype(BF), (0, 0)).astype(BF)

    def by_member(work, h):
        for e in range(piece_members):
            work(h * piece_members + e)

    kv_rows = piece_members * slots
    for h in range(PIECES):
        finish_rows[h]()
        arrived = arrived_s[h * wire_rows:(h + 1) * wire_rows, :]
        latent = jnp.concatenate(
            [dot(orders[p], arrived, (1, 0)).astype(BF) for p in range(PIECES)], axis=1
        )
        for c in range(0, 2 * width, 512):
            kv_s[h * kv_rows:(h + 1) * kv_rows, c:c + 512] = dot(
                latent, kvw_s[:, c:c + 512], (1, 0)
            ).astype(BF)
        by_member(attend, h)
    pred_s[0:fields, :] = dot(fw_ref[...], att_s[...], (1, 0))
    if padded > fields:
        pred_s[fields:padded, :] = jnp.zeros((padded - fields, members * points), F32)

    area = area_ref[...]
    almost_fair = 1.0 - (1.0 - FAIRNESS) / members
    spread_factor = almost_fair / (members * (members - 1))

    def judge(i, total):
        fs = part(i, 8)
        goal = target_s[fs, :]
        preds = [pred_s[fs, e * points:(e + 1) * points] for e in range(members)]
        slopes = []
        skill = jnp.zeros((8, points), F32)
        for e in range(members):
            u = preds[e] - goal
            v = u * u + SMOOTHING
            r = lax.rsqrt(v)
            skill += v * r
            slopes.append(u * r * (1.0 / members))
        spread = jnp.zeros((8, points), F32)
        pulls = [jnp.zeros((8, points), F32) for _ in range(members)]
        for a in range(members):
            for b in range(a + 1, members):
                u = preds[a] - preds[b]
                v = u * u + SMOOTHING
                r = lax.rsqrt(v)
                spread += v * r
                w = u * r
                pulls[a] = pulls[a] + w
                pulls[b] = pulls[b] - w
        pointwise = skill * (1.0 / members) - spread_factor * spread
        valid = iota((8, points), 0) + i * 8 < fields
        for e in range(members):
            dp_s[fs, e * points:(e + 1) * points] = (slopes[e] - spread_factor * pulls[e]) * area
        return total + jnp.where(valid, pointwise * area, 0.0)

    total_s[...] = lax.fori_loop(0, padded // 8, judge, jnp.zeros((8, points), F32))
    finish_total = exchange(shards, me, 8, total_s, totals_s, total_send, total_recv, whole=True)
    totals_s[part(me, 8), :] = total_s[...]

    dp = dp_s[0:fields, :].astype(BF)
    for k in range(groups):
        cs = slice(k * 256, (k + 1) * 256)
        da_s[cs, :] = dot(fw_ref[:, cs], dp, (0, 0)).astype(BF)

    def fold(product):
        kept = (product * head_mask).reshape(group_heads, slots, 256)
        return jnp.sum(kept, axis=0).astype(BF)

    def backward(e):
        rs, gs = part(e, slots), part(e, points)
        for k in range(groups):
            cs = slice(k * 256, (k + 1) * 256)
            vs = slice(width + k * 256, width + (k + 1) * 256)
            values = blocks(kv_s[rs, vs])
            weight = p_s[e, k]
            da = da_s[cs, gs]
            dw = dot(values, da, (1, 0))
            pull = (weight * dw).reshape(group_heads, slots, points)
            mean = jnp.sum(pull, axis=1, keepdims=True)
            ds = pull - weight.reshape(group_heads, slots, points) * mean
            ds = (ds.reshape(hs, points) * scale).astype(BF)
            sg_s[rs, cs] = fold(dot(ds, q_s[gs, cs], (1, 0)))
            sg_s[rs, vs] = fold(dot(weight.astype(BF), da, (1, 1)))

    finish_back = []
    for h in range(PIECES):
        by_member(backward, h)
        ws = slice(h * wire_rows, (h + 1) * wire_rows)
        latent_grad = dot(sg_s[h * kv_rows:(h + 1) * kv_rows, :], kvw_s[...], (1, 1)).astype(BF)
        sent = jnp.zeros((wire_rows, wide), F32)
        for p in range(PIECES):
            sent += dot(orders[p], latent_grad[:, p * wide:(p + 1) * wide], (0, 0))
        grads_s[ws, :] = sent.astype(BF)
        finish_back.append(exchange(
            shards, me, per, grads_s.at[ws], back_s.at[ws], back_send, back_recv, base=h * shards
        ))
        own = part(me + h * shards, per)
        back_s[own, :] = grads_s[own, :]
    finish_total()
    loss_ref[...] = jnp.full(loss_ref.shape, 1.0, F32) * (jnp.sum(totals_s[...]) / count)
    for h in range(PIECES):
        finish_back[h]()
        back = back_s[h * wire_rows:(h + 1) * wire_rows, :]
        for p in range(PIECES):
            out_ref[h * piece_rows:(h + 1) * piece_rows, p * wide:(p + 1) * wide] = dot(
                selects[p], back, (0, 0)
            ).astype(BF)


def decode(ask, mesh_rows, x, query_weight, kv_weight, field_weight, target, area, edge_slot, shards, members, cap):
    fields, points = target.shape
    width = mesh_rows.shape[1]
    nodes = mesh_rows.shape[0] // members
    slots = shards * cap
    rows = members * slots
    padded = -(-fields // 8) * 8
    group_heads = 256 * HEADS // width
    vmem = pl.BlockSpec(memory_space=pltpu.VMEM)
    hbm = pl.BlockSpec(memory_space=pl.ANY)
    sems = pltpu.SemaphoreType.DMA((shards,))
    piece_sems = pltpu.SemaphoreType.DMA((PIECES * shards,))
    count = float(fields * points * shards)
    return pl.pallas_call(
        functools.partial(decoder_kernel, shards, members, fields, slots, cap, nodes, count),
        out_shape=(
            jax.ShapeDtypeStruct(mesh_rows.shape, BF),
            jax.ShapeDtypeStruct((1, 1), F32),
        ),
        in_specs=[vmem] * 6 + [hbm] * 3,
        out_specs=(vmem, vmem),
        scratch_shapes=[
            pltpu.VMEM(x.shape, BF),
            pltpu.VMEM(query_weight.shape, BF),
            pltpu.VMEM(kv_weight.shape, BF),
            pltpu.VMEM(ask.shape, jnp.int32),
            pltpu.VMEM((PIECES * rows, width // PIECES), BF),
            pltpu.VMEM((PIECES * rows, width // PIECES), BF),
            pltpu.VMEM((PIECES * rows, width // PIECES), BF),
            pltpu.VMEM((PIECES * rows, width // PIECES), BF),
            pltpu.VMEM((8, points), F32),
            pltpu.VMEM((shards * 8, points), F32),
            pltpu.VMEM((members * points, width), BF),
            pltpu.VMEM((rows, 2 * width), BF),
            pltpu.VMEM((members, HEADS // group_heads, group_heads * slots, points), F32),
            pltpu.VMEM((width, members * points), BF),
            pltpu.VMEM((padded, points), F32),
            pltpu.VMEM((padded, members * points), F32),
            pltpu.VMEM((padded, members * points), F32),
            pltpu.VMEM((width, members * points), BF),
            pltpu.VMEM((rows, 2 * width), BF),
        ] + [sems] * 2 + [piece_sems] * 4 + [sems] * 2 + [pltpu.SemaphoreType.DMA((3,))],
        compiler_params=pltpu.CompilerParams(
            collective_id=0, has_side_effects=True, vmem_limit_bytes=60 * 1024 * 1024
        ),
    )(ask, mesh_rows, field_weight, target, area, edge_slot, x, query_weight, kv_weight)


def local(
    grid_latent, mesh_latent, query_weight, kv_weight, field_weight, target, area_weight, request, edge_slot,
):
    members, points, width = grid_latent.shape
    nodes = mesh_latent.shape[1]
    shards = lax.axis_size("space")
    cap = request.shape[2]
    slots = shards * cap
    per = cap * members
    ask = jnp.broadcast_to(
        request.reshape(shards, 1, cap, 1, 1), (shards, PIECES, cap, members // PIECES, 128)
    ).reshape(shards * per, 128)
    mesh_grad, loss = decode(
        ask, mesh_latent.reshape(members * nodes, width), grid_latent.reshape(members * points, width),
        query_weight, kv_weight, field_weight, target, area_weight.reshape(1, points), edge_slot,
        shards, members, cap,
    )
    mesh_grad = mesh_grad.reshape(members, nodes, width)
    mean_loss = loss.reshape(1)
    return (mesh_grad, mean_loss)


def solution(mesh):
    placed = (
        P(None, ("groups", "space"), None),
        P(None, ("groups", "space"), None),
        P(),
        P(),
        P(),
        P(None, ("groups", "space")),
        P(("groups", "space")),
        P(("groups", "space"), None, None),
        P(None, ("groups", "space")),
    )
    return jax.shard_map(
        local,
        mesh=mesh,
        in_specs=placed,
        out_specs=(P(None, ("groups", "space"), None), P("groups")),
        check_vma=False,
    )
```
